32 devices in a mesh: dp: 8 (over y, x, core), tm: 4 (over z).
Axes of the slice: x: 2, y: 2, z: 4, core: 2. Of those that a mesh axis runs over, the one named last changes fastest.
Arguments:
- inputs: bfloat16 [4, 8, 1536, 512], P(None, 'dp', 'tm'), may hold values from -6 to 6
- utterance_ids: int32 [4, 8, 1536], P(None, 'dp', 'tm'), may hold values from -1 to 3, as said below
- cotangent: bfloat16 [4, 8, 1536, 512], P(None, 'dp', 'tm'), may hold values from -6 to 6
- pointwise: float32 [6, 512, 512], P(None, ('dp', 'tm'))
- pointwise_first: float32 [6, 512, 512], P(None, ('dp', 'tm'))
- pointwise_second: float32 [6, 512, 512], P(None, ('dp', 'tm')), may hold values from 3072 to 12288
- depthwise: float32 [5, 5, 512], replicated, may hold values from -2.5 to 2.5
- depthwise_first: float32 [5, 5, 512], replicated
- depthwise_second: float32 [5, 5, 512], replicated, may hold values from 3072 to 12288
- norm_affine: float32 [2, 5, 512], replicated
- norm_first: float32 [2, 5, 512], replicated
- norm_second: float32 [2, 5, 512], replicated, may hold values from 3072 to 12288
- excite_mats: float32 [2, 64, 512], replicated
- excite_first: float32 [2, 64, 512], replicated
- excite_second: float32 [2, 64, 512], replicated, may hold values from 3072 to 12288
Outputs:
- block_out: bfloat16 [4, 8, 1536, 512], P(None, 'dp', 'tm')
- input_grad: float32 [4, 8, 1536, 512], P(None, 'dp', 'tm')
- pointwise_moment: float32 [6, 512, 512], P(None, ('dp', 'tm'))
- pointwise_square: float32 [6, 512, 512], P(None, ('dp', 'tm'))
- pointwise_new: float32 [6, 512, 512], P(None, ('dp', 'tm'))
- pointwise_half: bfloat16 [6, 512, 512], P(None, ('dp', 'tm'))
- depthwise_moment: float32 [5, 5, 512], replicated
- depthwise_square: float32 [5, 5, 512], replicated
- depthwise_new: float32 [5, 5, 512], replicated
- norm_moment: float32 [2, 5, 512], replicated
- norm_square: float32 [2, 5, 512], replicated
- norm_new: float32 [2, 5, 512], replicated
- excite_moment: float32 [2, 64, 512], replicated
- excite_square: float32 [2, 64, 512], replicated
- excite_new: float32 [2, 64, 512], replicated
- trust_norms: float32 [2, 23], replicated
The draws below stay inside these ranges and needn't reach their ends.
Inputs may be any that keep to these rules, and one draw needn't show every extreme that they name: `utterance_ids`: -1 marks padding. Along a row the ids other than -1 never fall; every row holds each id 0 to 3 in one unbroken run of frames. In one row of each micro-batch, chosen by the seed, utterance 1 begins exactly at frame 1536 // 2.
All inputs are finite; a program needn't handle non-finite values.
Results may differ from the reference program's by a relative error of at most 0.024.
The reference program's roundings to bfloat16 on the way count: a program that leaves them out, or rounds other values in their place, can miss the bound.
Values may be sent and summed in bfloat16 or wider, within the bound.
No kernel may reach another device: no remote copies, remote signals or barrier semaphores. Data moves between devices by JAX's collectives and lax.ppermute only.
A program may use at most 192 MiB of HBM per device.

```python
import math
import jax
import jax.numpy as jnp
from jax import lax

C = 512
SEW = 64
K = 5
NCONV = 5
NSEG = 4
MB = 4
STEP = 5
FR = 384
NPW = 6
ROWS = 8
LEN = 1536


def first_moment(key, dims):
    return jax.random.normal(key, dims, jnp.float32) * (jnp.sqrt(jnp.float32(MB * ROWS * LEN)) / 4.0)


def draw_utterance_ids(key, part):
    key = jax.random.fold_in(key, 7)
    keys = jax.random.split(key, 6)
    dims = (MB, ROWS, 1)
    start = jax.random.randint(keys[0], dims, FR // 4, 3 * FR // 4 + 1)
    finish_wide = jax.random.randint(keys[1], dims, LEN - FR + FR // 4, LEN - FR // 2 + 1)
    chosen = jax.random.randint(keys[5], (MB, 1, 1), 0, ROWS)
    rows_here = jnp.arange(ROWS, dtype=jnp.int32)[None, :, None]
    finish = jnp.where(rows_here == chosen, LEN // 2, finish_wide)
    tail = jax.random.randint(keys[2], dims, 0, FR // 8 + 1)
    stop = LEN - tail
    first_cut = finish + 1 + jax.random.randint(keys[3], dims, 0, stop - finish - 2)
    second_cut = first_cut + 1 + jax.random.randint(keys[4], dims, 0, stop - first_cut - 1)
    places = jnp.arange(LEN, dtype=jnp.int32)[None, None, :]
    labels = (places >= finish).astype(jnp.int32) + (places >= first_cut).astype(jnp.int32) + (places >= second_cut).astype(jnp.int32)
    return jnp.where((places < start) | (places >= stop), -1, labels).astype(jnp.int32)


def draw_pointwise(key, part):
    key = jax.random.fold_in(key, 23)
    base_key, rough_key = jax.random.split(key)
    place = jnp.arange(C, dtype=jnp.float32) / C
    rising = jnp.exp(jnp.log(3.0) * (place - 0.5))
    rough = jax.random.uniform(rough_key, (NPW, C, 1), jnp.float32, 0.7, 1.4)
    base = jax.random.normal(base_key, (NPW, C, C), jnp.float32) / jnp.sqrt(jnp.float32(C))
    return base * rising[None, :, None] * rough


def draw_pointwise_first(key, part):
    key = jax.random.fold_in(key, 11)
    return first_moment(key, (NPW, C, C))


def draw_depthwise_first(key, part):
    key = jax.random.fold_in(key, 13)
    return first_moment(key, (NCONV, K, C))


def draw_norm_first(key, part):
    key = jax.random.fold_in(key, 17)
    return first_moment(key, (2, NCONV, C))


def draw_excite_first(key, part):
    key = jax.random.fold_in(key, 19)
    return first_moment(key, (2, SEW, C))


def draw_norm_affine(key, part):
    key = jax.random.fold_in(key, 3)
    rough_key, shift_key = jax.random.split(key)
    place = jnp.arange(C, dtype=jnp.float32) / C
    rising = jnp.exp(jnp.log(3.0) * (place - 0.5))
    rough = jax.random.uniform(rough_key, (NCONV, C), jnp.float32, 0.7, 1.4)
    gains = rising[None, :] * rough
    shifts = 0.3 * jax.random.normal(shift_key, (NCONV, C), jnp.float32)
    return jnp.stack([gains, shifts])


def draw_excite_mats(key, part):
    key = jax.random.fold_in(key, 5)
    down_key, up_key = jax.random.split(key)
    down = jax.random.normal(down_key, (SEW, C), jnp.float32) / jnp.sqrt(jnp.float32(C))
    upward = 2.0 * jax.random.normal(up_key, (SEW, C), jnp.float32) / jnp.sqrt(jnp.float32(SEW))
    return jnp.stack([down, upward])


def level_of(rng, shape, cuts, least, top_value):
    gain, own = 1.0, jax.random.fold_in(rng, 6)
    for axis_at, parts in cuts:
        draws = jnp.exp(jax.random.uniform(jax.random.fold_in(own, axis_at), (parts,), jnp.float32, least / len(cuts), top_value / len(cuts)))
        gain = gain * jnp.repeat(draws, shape[axis_at] // parts).reshape([-1 if axis == axis_at else 1 for axis in range(len(shape))])
    return gain


def normal_values(key, shape, width, bound, cuts=(), held_as=jnp.bfloat16):
    values = jax.random.normal(key, shape, jnp.float32) * width
    if len(cuts) > 0:
        values = level_of(key, shape, cuts, -0.22, 0.18) * values
    return jnp.clip(values, min=-bound, max=bound).astype(held_as)


def setup_inputs(seed: int = 0) -> dict:
    key_of = jax.random.split(jax.random.key(seed), 16)
    inputs = normal_values(key_of[0], (MB, ROWS, LEN, C), 1.0, 6.0, ((1, 8), (2, 4)))
    utterance_ids = draw_utterance_ids(jax.random.fold_in(key_of[15], 71), 0)
    cotangent = normal_values(key_of[2], (MB, ROWS, LEN, C), 1.0, 6.0, ((1, 8), (2, 4)))
    pointwise = draw_pointwise(jax.random.fold_in(key_of[15], 71), 0)
    pointwise_first = draw_pointwise_first(jax.random.fold_in(key_of[15], 71), 0)
    pointwise_second = jnp.clip(jnp.exp(math.log(12288.0) - 1.3862944 * jax.random.uniform(key_of[5], (NPW, C, C), jnp.float32) ** level_of(key_of[5], (NPW, C, C), ((1, 32),), -0.2, 0.2)), 3072.0, 12288.0)
    depthwise = normal_values(key_of[6], (NCONV, K, C), K ** -0.5, 2.5, (), jnp.float32)
    depthwise_first = draw_depthwise_first(jax.random.fold_in(key_of[15], 71), 0)
    depthwise_second = jnp.clip(jnp.exp(jax.random.uniform(key_of[8], (NCONV, K, C), jnp.float32, math.log(3072.0), math.log(12288.0))), 3072.0, 12288.0)
    norm_affine = draw_norm_affine(jax.random.fold_in(key_of[15], 71), 0)
    norm_first = draw_norm_first(jax.random.fold_in(key_of[15], 71), 0)
    norm_second = jnp.clip(jnp.exp(jax.random.uniform(key_of[11], (2, NCONV, C), jnp.float32, math.log(3072.0), math.log(12288.0))), 3072.0, 12288.0)
    excite_mats = draw_excite_mats(jax.random.fold_in(key_of[15], 71), 0)
    excite_first = draw_excite_first(jax.random.fold_in(key_of[15], 71), 0)
    excite_second = jnp.clip(jnp.exp(jax.random.uniform(key_of[14], (2, SEW, C), jnp.float32, math.log(3072.0), math.log(12288.0))), 3072.0, 12288.0)
    return {"inputs": inputs, "utterance_ids": utterance_ids, "cotangent": cotangent, "pointwise": pointwise, "pointwise_first": pointwise_first, "pointwise_second": pointwise_second, "depthwise": depthwise, "depthwise_first": depthwise_first, "depthwise_second": depthwise_second, "norm_affine": norm_affine, "norm_first": norm_first, "norm_second": norm_second, "excite_mats": excite_mats, "excite_first": excite_first, "excite_second": excite_second}


HIGHEST = lax.Precision.HIGHEST
BN_EPS = 1e-05
BETA_ONE = 0.5
BETA_TWO = 0.5
LAMB_EPS = 1e-06
DECAY = 0.01
RATE = 1.0

@jax.custom_vjp
def low(v):
    return lax.optimization_barrier(v.astype(jnp.bfloat16)).astype(jnp.float32)

@jax.custom_vjp
def low_back(v):
    return v

def low_keep(v):
    return (low(v), None)

def low_pass(kept, grad):
    return (grad,)

def back_keep(v):
    return (v, None)

def back_low(kept, grad):
    return (low(grad),)
low.defvjp(low_keep, low_pass)
low_back.defvjp(back_keep, back_low)

def swish_act(value):
    return value * jax.nn.sigmoid(value)

def block_forward(inputs, pointwise, depthwise, norm_affine, excite_mats, utterance):
    frames = inputs.shape[1]
    live_mask = (utterance >= 0).astype(jnp.float32)[..., None]
    shifted = utterance + 1
    padded_ids = jnp.pad(shifted, ((0, 0), (2, 2)))
    linked = [((padded_ids[:, offset:offset + frames] == shifted) & (utterance >= 0)).astype(jnp.float32)[..., None] for offset in range(K)]
    frame_total = jnp.sum(live_mask)
    weights_low = low(pointwise)
    inputs_low = low(inputs)
    hidden = inputs_low
    for layer in range(NCONV):
        hidden_low = inputs_low if layer == 0 else low(hidden)
        padded = jnp.pad(hidden_low, ((0, 0), (2, 2), (0, 0)))
        mixed = jnp.zeros_like(hidden_low)
        for offset in range(K):
            mixed = mixed + depthwise[layer, offset] * padded[:, offset:offset + frames] * linked[offset]
        mixed = low_back(mixed)
        point = low_back(jnp.einsum('rtc,cd->rtd', low(mixed), weights_low[layer], precision=HIGHEST))
        average = lax.optimization_barrier(jnp.sum(point * live_mask, axis=(0, 1))) / frame_total
        variance = lax.optimization_barrier(jnp.sum(point * point * live_mask, axis=(0, 1))) / frame_total - average * average
        normed = (point - average) * lax.rsqrt(variance + BN_EPS)
        hidden = swish_act(norm_affine[0, layer] * normed + norm_affine[1, layer]) * live_mask
    onehot = (utterance[..., None] == jnp.arange(NSEG, dtype=jnp.int32)).astype(jnp.float32)
    segment_sums = jnp.einsum('rts,rtc->rsc', onehot, hidden, precision=HIGHEST)
    frame_counts = lax.optimization_barrier(jnp.sum(onehot, axis=1))
    pooled = segment_sums / frame_counts[..., None]
    excite_low = low(excite_mats)
    squeeze = low_back(jnp.einsum('rsc,jc->rsj', low(pooled), excite_low[0], precision=HIGHEST))
    excite = low_back(jnp.einsum('rsj,jc->rsc', low(swish_act(squeeze)), excite_low[1], precision=HIGHEST))
    gating = jax.nn.sigmoid(excite)
    spread = jnp.einsum('rts,rsc->rtc', onehot, gating, precision=HIGHEST)
    residual = low_back(jnp.einsum('rtc,cd->rtd', inputs_low, weights_low[NCONV], precision=HIGHEST))
    return swish_act(hidden * spread + residual) * live_mask

def lamb_update(weights, first, second, grads, axes):
    first_new = BETA_ONE * first + (1.0 - BETA_ONE) * grads
    second_new = BETA_TWO * second + (1.0 - BETA_TWO) * grads * grads
    first_hat = first_new / (1.0 - BETA_ONE ** STEP)
    second_hat = second_new / (1.0 - BETA_TWO ** STEP)
    update = first_hat / (jnp.sqrt(second_hat) + LAMB_EPS) + DECAY * weights
    weight_norm = jnp.sqrt(lax.optimization_barrier(jnp.sum(weights * weights, axis=axes, keepdims=True)))
    update_norm = jnp.sqrt(lax.optimization_barrier(jnp.sum(update * update, axis=axes, keepdims=True)))
    weights_new = weights - RATE * (weight_norm / update_norm) * update
    return (first_new, second_new, weights_new, weight_norm.reshape(-1), update_norm.reshape(-1))

def reference(inputs, utterance_ids, cotangent, pointwise, pointwise_first, pointwise_second, depthwise, depthwise_first, depthwise_second, norm_affine, norm_first, norm_second, excite_mats, excite_first, excite_second):

    def one_batch(carry, pieces):
        batch_in, batch_ids, batch_cot = pieces

        def forward(xin, pw_in, dw_in, nm_in, se_in):
            return block_forward(xin, pw_in, dw_in, nm_in, se_in, batch_ids)
        result, pull = jax.vjp(forward, batch_in.astype(jnp.float32), pointwise, depthwise, norm_affine, excite_mats)
        grads = pull(batch_cot.astype(jnp.float32))
        carry = tuple((total + piece for total, piece in zip(carry, grads[1:])))
        return (carry, (result.astype(jnp.bfloat16), grads[0]))
    zeros = (jnp.zeros_like(pointwise), jnp.zeros_like(depthwise), jnp.zeros_like(norm_affine), jnp.zeros_like(excite_mats))
    sums, stacked = lax.scan(one_batch, zeros, (inputs, utterance_ids, cotangent))
    block_out, input_grad = stacked
    grad_point, grad_depth, grad_norm, grad_excite = sums
    pw_moment, pw_square, pw_new, pw_wn, pw_un = lamb_update(pointwise, pointwise_first, pointwise_second, grad_point, (1, 2))
    dw_moment, dw_square, dw_new, dw_wn, dw_un = lamb_update(depthwise, depthwise_first, depthwise_second, grad_depth, (1, 2))
    nm_moment, nm_square, nm_new, nm_wn, nm_un = lamb_update(norm_affine, norm_first, norm_second, grad_norm, (2,))
    se_moment, se_square, se_new, se_wn, se_un = lamb_update(excite_mats, excite_first, excite_second, grad_excite, (1, 2))
    trust_norms = jnp.stack([jnp.concatenate([pw_wn, dw_wn, nm_wn, se_wn]), jnp.concatenate([pw_un, dw_un, nm_un, se_un])])
    return (block_out, input_grad, pw_moment, pw_square, pw_new, pw_new.astype(jnp.bfloat16), dw_moment, dw_square, dw_new, nm_moment, nm_square, nm_new, se_moment, se_square, se_new, trust_norms)
```

```python
import functools

import jax
import jax.numpy as jnp
from jax import lax
from jax.experimental import pallas as pl
from jax.experimental.pallas import tpu as pltpu
from jax.sharding import PartitionSpec as P

NSEG = 4
STEP = 5


BN_EPS = 1e-05
BETA_ONE = 0.5
BETA_TWO = 0.5
LAMB_EPS = 1e-06
DECAY = 0.01
RATE = 1.0
REACH = 2
LANES = 128
ROWS8 = 8
STRIP = 16
WIDE = 4
BLOCK = 256
EDGE = 16
SEGROWS = 16
SCOPED = 56 * 1024 * 1024
F32 = jnp.float32
LOW = jnp.bfloat16
SIDES = (0, 1, 3, 4)


def col(chunk):
    return slice(chunk * LANES, (chunk + 1) * LANES)


def block_rows(block):
    return pl.ds(pl.multiple_of(block * BLOCK, BLOCK), BLOCK)


def strip_rows(index, margin=0):
    return pl.ds(pl.multiple_of(index * STRIP, STRIP), STRIP + 2 * margin)


def middle_rows(index):
    return pl.ds(pl.multiple_of(index * STRIP + EDGE, STRIP), STRIP)


def low_dot(left, right, dims=((1,), (0,))):
    return lax.dot_general(left, right, (dims, ((), ())), preferred_element_type=F32)


def rounded(value):
    return value.astype(LOW).astype(F32)


def tiles(value):
    return value.reshape(-1, ROWS8, value.shape[-1])


def flat(value):
    return value.reshape(-1, value.shape[-1])


def fold(value):
    return jnp.sum(tiles(value), axis=0)


def eight(value):
    return jnp.broadcast_to(value, (ROWS8, value.shape[-1]))


def two_parts(value):
    high = value.astype(LOW)
    return high, (value - high.astype(F32)).astype(LOW)


def three_parts(value):
    high = value.astype(LOW)
    value = value - high.astype(F32)
    middle = value.astype(LOW)
    return jnp.concatenate([high, middle, (value - middle.astype(F32)).astype(LOW)], axis=0)


def summed(ref):
    total = ref[0]
    for index in range(1, ref.shape[0]):
        total = total + ref[index]
    return total


def strips_of(block, strip, carry=0):
    count = BLOCK // STRIP
    return lax.fori_loop(
        0, count, lambda index, value: strip(block * count + index, value), carry, unroll=4
    )


def unrolled_strips_of(block, strip, carry=0):
    count = BLOCK // STRIP
    for index in range(count):
        carry = strip(block * count + index, carry)
    return carry


def wide_strips_of(block, wide_strip):
    count = BLOCK // (STRIP * WIDE)
    lax.fori_loop(0, count, lambda index, carry: wide_strip(block * count + index, carry), 0)


def over_blocks(length, body, carry=0):
    return lax.fori_loop(0, length // BLOCK, body, carry)


def wrap_edges(buffer, chunks, length):
    for chunk in range(chunks):
        for tile in range(2):
            low, high = tile * ROWS8, (tile + 1) * ROWS8
            ends = buffer[chunk, length + low : length + high, :]
            buffer[chunk, low:high, :] = pltpu.roll(ends, 1, 0)
            starts = buffer[chunk, EDGE + low : EDGE + high, :]
            buffer[chunk, EDGE + length + low : EDGE + length + high, :] = pltpu.roll(
                starts, ROWS8 - 1, 0
            )


def into_order(sources, starts, target, chunks, length, edge):
    run = length // ROWS8

    def some(index, carry):
        for source, start in zip(sources, starts, strict=True):
            for part in range(source.shape[0] // run):
                for chunk in range(chunks):
                    rows = pl.ds(pl.multiple_of(part * run + index * 16, 16), 16)
                    value = source[rows, col(chunk)].astype(F32)
                    first = index * 128 + (start + (edge + part))
                    target[chunk, pl.ds(first, 16, stride=ROWS8), :] = value
        return carry

    lax.fori_loop(0, run // 16, some, 0)


def out_of_order(source, target, chunks, length, edge):
    run = length // ROWS8

    def some(index, carry):
        for sublane in range(ROWS8):
            for chunk in range(chunks):
                value = source[chunk, pl.ds(index * 128 + (edge + sublane), 16, stride=ROWS8), :]
                rows = pl.ds(pl.multiple_of(sublane * run + index * 16, 16), 16)
                target[rows, col(chunk)] = value.astype(LOW)
        return carry

    lax.fori_loop(0, run // 16, some, 0)


def send_pieces(me, source, targets, sems):
    count = len(targets)
    size = source.shape[0] // count
    copies = []
    for place in range(count):
        rows = pl.ds(place * size, size)
        step = lax.rem(place - me + count, count) if count > 1 else 0
        for k, target in enumerate(targets):
            copy = pltpu.make_async_copy(source.at[rows], target, sems.at[place])
            if count == 1:
                copy.start()
            else:
                pl.when(step == k)(copy.start)
        copies.append(copy)
    return copies


def write_copies(ref, tops, bottoms):
    for index in range(ref.shape[0]):
        for row, value in enumerate(tops + bottoms):
            ref[index, row : row + 1, :] = value


def norm_terms(stats, inv_total, norm, layer, chunks, par):
    halves = []
    for chunk in range(chunks):
        mean = stats[chunk : chunk + 1] * inv_total
        second = stats[chunks + chunk : chunks + chunk + 1] * inv_total
        inv_std = lax.rsqrt(second - mean * mean + BN_EPS)
        gain = 0.5 * norm[0, layer : layer + 1, col(chunk)] * inv_std
        shift = 0.5 * norm[1, layer : layer + 1, col(chunk)] - mean * gain
        par[0:1, col(chunk)] = mean
        par[1:2, col(chunk)] = inv_std
        par[2:3, col(chunk)] = gain
        par[3:4, col(chunk)] = shift
        halves.append((eight(gain), eight(shift)))
    return halves


def of_stack(matrix_ref, slot):
    return matrix_ref if slot is None else matrix_ref.at[slot]


class Blocks:
    def __init__(self, source, target, sems):
        self.source, self.target, self.sems = source, target, sems
        self.count = source.shape[0] // BLOCK

    def copy(self, block):
        rows = block_rows(block)
        return pltpu.make_async_copy(self.source.at[rows], self.target.at[rows], self.sems.at[block])

    def start(self, block):
        self.copy(block).start()

    def wait(self, block):
        self.copy(block).wait()

    def start_all(self):
        for block in range(self.count):
            self.start(block)
        return self

    def wait_all(self):
        for block in range(self.count):
            self.wait(block)


def bring(sources, targets, sems):
    copies = [
        pltpu.make_async_copy(source, target, sems.at[index])
        for index, (source, target) in enumerate(zip(sources, targets, strict=True))
    ]
    for copy in copies:
        copy.start()
    return copies


def same_utterance(codes, index):
    code = tiles(codes[strip_rows(index, EDGE), :])
    return [code[k : k + 2] == code[2:4] for k in SIDES]


def forward_rest(
    length, channels, layer, codes, depth, taps, buffer, mixed, matrix, point, outs, copies, own
):
    chunks = channels // LANES
    wrap_edges(buffer, chunks, length)
    for k in range(5):
        taps[k] = eight(depth[layer, k : k + 1, :])

    def strip(index, carry):
        same = same_utterance(codes, index)
        for chunk in range(chunks):
            value = tiles(buffer[chunk, strip_rows(index, EDGE), :])
            total = taps[REACH, :, col(chunk)] * value[2:4]
            for slot, k in enumerate(SIDES):
                beside = jnp.where(same[slot], value[k : k + 2], 0.0)
                total = total + taps[k, :, col(chunk)] * beside
            mixed[strip_rows(index), col(chunk)] = flat(total).astype(LOW)
        return carry

    def multiply(block, carry):
        rows = block_rows(block)
        product = low_dot(mixed[rows, :], matrix[...])
        point[rows, :] = product
        if own is not None:
            product = product * own[rows, 0:1]
        return carry[0] + fold(product), carry[1] + fold(product * product)

    def block_step(block, carry):
        carry = multiply(block - 1, carry)
        unrolled_strips_of(block, strip)
        outs[1].start(block - 1)
        outs[0].start(block)
        return carry

    zero = jnp.zeros((ROWS8, channels), F32)
    blocks = length // BLOCK
    strips_of(0, strip)
    outs[0].start(0)
    carry = lax.fori_loop(1, blocks, block_step, (zero, zero))
    first, second = multiply(blocks - 1, carry)
    outs[1].start(blocks - 1)
    first = jnp.sum(first, axis=0, keepdims=True)
    second = jnp.sum(second, axis=0, keepdims=True)
    write_copies(
        copies,
        [first[:, col(chunk)] for chunk in range(chunks)],
        [second[:, col(chunk)] for chunk in range(chunks)],
    )


def send_whole(pairs, sems):
    copies = bring([pair[0] for pair in pairs], [pair[1] for pair in pairs], sems)
    for copy in copies:
        copy.wait()


def piece_starts(me_ref, count):
    if count == 1:
        return [0]
    me = me_ref[0]
    return [lax.rem(me - k + count, count) * (ROWS8 // count) for k in range(count)]


def first_kernel(halo, count, me_ref, *rest):
    x_refs, rest = rest[:count], rest[count:]
    codes_ref, matrix_ref, depth_ref = rest[:3]
    rest = rest[3:]
    own_ref = rest[0] if halo else None
    rest = rest[1:] if halo else rest
    mixed_ref, point_ref, order_ref, copies_ref = rest[:4]
    x, codes, order, depth, copies, taps, matrix, mixed, point, buffer = rest[4:14]
    in_sems, out_sems, whole_sems, last_sems = rest[14:18]
    length, channels = order.shape
    chunks = channels // LANES
    xs = [x.at[pl.ds(k * (length // count), length // count)] for k in range(count)]
    x_in = bring(x_refs, xs, in_sems)
    own = rest[18] if halo else None
    brought = bring(
        [codes_ref, depth_ref, matrix_ref] + ([own_ref] if halo else []),
        [codes, depth, matrix] + ([own] if halo else []),
        whole_sems,
    )
    brought[0].wait()
    for copy in x_in:
        copy.wait()
    into_order(xs, piece_starts(me_ref, count), buffer, chunks, length, EDGE)
    outs = [Blocks(mixed, mixed_ref, out_sems.at[0]), Blocks(point, point_ref, out_sems.at[1])]
    order_out = Blocks(order, order_ref, out_sems.at[2])

    def fill(block, carry):
        def strip(index, carry):
            live = codes[middle_rows(index), :] >= 0.0
            for chunk in range(chunks):
                value = jnp.where(live, buffer[chunk, middle_rows(index), :], 0.0)
                buffer[chunk, middle_rows(index), :] = value
                order[strip_rows(index), col(chunk)] = value.astype(LOW)
            live = live.astype(F32)
            if own is not None:
                live = live * own[strip_rows(index), :]
            return carry + fold(live)

        carry = unrolled_strips_of(block, strip, carry)
        order_out.start(block)
        return carry

    for copy in brought[1:]:
        copy.wait()
    total = over_blocks(length, fill, jnp.zeros((ROWS8, LANES), F32))
    total = eight(jnp.sum(total, axis=0, keepdims=True))
    forward_rest(
        length,
        channels,
        0,
        codes,
        depth,
        taps,
        buffer,
        mixed,
        matrix,
        point,
        outs,
        copies.at[:, 0:ROWS8, :],
        own,
    )
    for index in range(copies.shape[0]):
        copies[index, ROWS8 : 2 * ROWS8, :] = total
    send_whole([(copies, copies_ref)], last_sems)
    for out in outs + [order_out]:
        out.wait_all()


def next_kernel(
    halo,
    layer,
    slot,
    codes_ref,
    before_ref,
    matrix_ref,
    sums_ref,
    norm_ref,
    depth_ref,
    *rest,
):
    if layer > 0:
        inverse_ref, rest = rest[0], rest[1:]
    own_ref = rest[0] if halo else None
    rest = rest[1:] if halo else rest
    mixed_ref, point_ref, copies_ref, par_ref = rest[:4]
    rest = rest[4:]
    if layer == 0:
        inverse_out_ref = rest[0]
        rest = rest[1:]
    codes, before, sums, inverse, norm, par, depth, copies = rest[:8]
    taps, matrix, mixed, point, buffer = rest[8:13]
    in_sems, out_sems, whole_sems, last_sems = rest[13:17]
    own = rest[17] if halo else None
    length, channels = before_ref.shape
    chunks = channels // LANES
    brought = bring(
        [codes_ref, sums_ref, norm_ref] + ([inverse_ref] if layer > 0 else []),
        [codes, sums, norm] + ([inverse] if layer > 0 else []),
        whole_sems.at[0],
    )
    before_in = Blocks(before_ref, before, in_sems).start_all()
    later = bring(
        [depth_ref, of_stack(matrix_ref, slot)] + ([own_ref] if halo else []),
        [depth, matrix] + ([own] if halo else []),
        whole_sems.at[1],
    )
    for copy in brought[1:]:
        copy.wait()
    stats = summed(sums)
    if layer == 0:
        inverse[...] = eight(1.0 / stats[ROWS8 : ROWS8 + 1])
    halves = norm_terms(stats, inverse[0:1, :], norm, layer, chunks, par)
    brought[0].wait()

    def fill(block, carry):
        def strip(index, carry):
            live = codes[middle_rows(index), :] >= 0.0
            for chunk in range(chunks):
                gain, shift = halves[chunk]
                half = tiles(before[strip_rows(index), col(chunk)]) * gain + shift
                value = flat(half * jnp.tanh(half) + half)
                buffer[chunk, middle_rows(index), :] = rounded(jnp.where(live, value, 0.0))
            return carry

        before_in.wait(block)
        unrolled_strips_of(block, strip)
        return carry

    over_blocks(length, fill)
    for copy in later:
        copy.wait()
    outs = [Blocks(mixed, mixed_ref, out_sems.at[0]), Blocks(point, point_ref, out_sems.at[1])]
    forward_rest(
        length,
        channels,
        layer + 1,
        codes,
        depth,
        taps,
        buffer,
        mixed,
        matrix,
        point,
        outs,
        copies,
        own,
    )
    pairs = [(copies, copies_ref), (par, par_ref)]
    if layer == 0:
        pairs.append((inverse, inverse_out_ref))
    send_whole(pairs, last_sems)
    for out in outs:
        out.wait_all()


def squeeze_forward(segment, counts, excite_low):
    pooled_low = (segment / counts).astype(LOW)
    squeeze = low_dot(pooled_low, excite_low[0], ((1,), (1,)))
    half = 0.5 * squeeze
    turned = jnp.tanh(half)
    act = (half * turned + half).astype(LOW)
    gating = 0.5 * jnp.tanh(0.5 * low_dot(act, excite_low[1])) + 0.5
    slope = 0.5 * (1.0 + turned) * (1.0 + half * (1.0 - turned))
    return pooled_low, slope, act, gating


def by_segment(code, rows):
    value = rows[NSEG - 1]
    for index in reversed(range(NSEG - 1)):
        value = jnp.where(code == float(index), rows[index], value)
    return value


def excite_kernel(layer, count, slot, me_ref, *rest):
    cot_refs, rest = rest[:count], rest[count:]
    codes_ref, point_ref, x_ref, matrix_ref, sums_ref, inverse_ref, norm_ref = rest[:7]
    excite_ref = rest[7]
    rest = rest[8:]
    out_refs, rest = rest[:count], rest[count:]
    res_ref, affine_ref, copies_ref, excite_grad_ref, par_ref = rest[:5]
    codes, point, x, cot, matrix, sums, inverse, norm, excite = rest[5:14]
    hidden, residual, total, cot_order, out, res, copies, excite_grad, par = rest[14:23]
    held, sums_of, in_sems, out_sems, whole_sems, last_sems = rest[23:]
    length, channels = point_ref.shape
    chunks = channels // LANES
    first_ones = bring(
        [sums_ref, inverse_ref, norm_ref, codes_ref], [sums, inverse, norm, codes], whole_sems.at[0]
    )
    later = bring([of_stack(matrix_ref, slot), excite_ref], [matrix, excite], whole_sems.at[1])
    point_in = Blocks(point_ref, point, in_sems.at[0])
    x_in = Blocks(x_ref, x, in_sems.at[1])
    for block in range(point_in.count):
        point_in.start(block)
        x_in.start(block)
    cots = [cot.at[pl.ds(k * (length // count), length // count)] for k in range(count)]
    cot_in = bring(cot_refs, cots, in_sems.at[2])
    res_sender = Blocks(res, res_ref, out_sems.at[1])
    affine_sender = Blocks(residual, affine_ref, out_sems.at[2])
    for copy in first_ones[:-1]:
        copy.wait()
    halves = norm_terms(summed(sums), inverse[0:1, :], norm, layer, chunks, par)
    first_ones[-1].wait()
    later[0].wait()
    tile = jnp.zeros((ROWS8, LANES), F32)

    def pool(block, carry):
        def strip(index, carry):
            code = tiles(codes[middle_rows(index), :])
            rows = strip_rows(index)
            new = []
            for chunk in range(chunks):
                gain, shift = halves[chunk]
                half = tiles(point[rows, col(chunk)]) * gain + shift
                value = jnp.where(code >= 0.0, half * jnp.tanh(half) + half, 0.0)
                hidden[rows, col(chunk)] = flat(value)
                for segment in range(NSEG):
                    part = jnp.where(code == float(segment), value, 0.0)
                    new.append(carry[len(new)] + jnp.sum(part, axis=0))
            for segment in range(NSEG):
                part = jnp.where(code == float(segment), 1.0, 0.0)
                new.append(carry[len(new)] + jnp.sum(part, axis=0))
            return tuple(new)

        point_in.wait(block)
        x_in.wait(block)
        rows = block_rows(block)
        residual[rows, :] = low_dot(x[rows, :], matrix[...])
        return unrolled_strips_of(block, strip, carry)

    def hold(carry):
        held[...] = jnp.zeros(held.shape, F32)
        for chunk in range(chunks):
            for index in range(NSEG):
                value = jnp.sum(carry[chunk * NSEG + index], axis=0, keepdims=True)
                held[index : index + 1, col(chunk)] = value
        return held[...]

    pooled = over_blocks(length, pool, (tile,) * ((chunks + 1) * NSEG))
    counts = [jnp.sum(value, axis=0, keepdims=True) for value in pooled[chunks * NSEG :]]
    counts = counts + [jnp.ones((SEGROWS - NSEG, LANES), F32)]
    counts = jnp.concatenate(counts, axis=0)[:, 0:1]
    segment = hold(pooled)
    later[1].wait()
    pooled_low, slope_small, act, gating = squeeze_forward(segment, counts, excite)

    def rows_of(value):
        held[...] = value
        return [
            [eight(held[index : index + 1, col(chunk)]) for index in range(NSEG)]
            for chunk in range(chunks)
        ]

    gates = rows_of(gating)
    for copy in cot_in:
        copy.wait()
    into_order(cots, piece_starts(me_ref, count), cot_order, chunks, length, 0)

    def finish(block, carry):
        def wide_strip(index, carry):
            for chunk in range(chunks):
                found = [None] * NSEG
                for part in range(WIDE):
                    place = index * WIDE + part
                    rows = strip_rows(place)
                    code = tiles(codes[middle_rows(place), :])
                    live = code >= 0.0
                    kept = tiles(hidden[rows, col(chunk)])
                    half = kept * by_segment(code, gates[chunk]) + tiles(residual[rows, col(chunk)])
                    half = 0.5 * half
                    turned = jnp.tanh(half)
                    one = 1.0 + turned
                    value = half * one
                    slope = 0.5 * (one + value * (1.0 - turned))
                    grad = jnp.where(live, tiles(cot_order[chunk, rows, :]) * slope, 0.0)
                    cot_order[chunk, rows, :] = flat(jnp.where(live, value, 0.0))
                    total[rows, col(chunk)] = flat(grad)
                    res[rows, col(chunk)] = flat(grad).astype(LOW)
                    value = grad * kept
                    for k in range(NSEG):
                        new = jnp.sum(jnp.where(code == float(k), value, 0.0), axis=0)
                        found[k] = new if found[k] is None else found[k] + new
                for k in range(NSEG):
                    sums_of[k, :, col(chunk)] += found[k]
            return carry

        wide_strips_of(block, wide_strip)
        res_sender.start(block)
        return carry

    sums_of[...] = jnp.zeros(sums_of.shape, F32)
    over_blocks(length, finish)
    grad_gating = hold(
        [sums_of[k, :, col(chunk)] for chunk in range(chunks) for k in range(NSEG)]
    )
    out_of_order(cot_order, out, chunks, length, 0)
    out_copies = send_pieces(me_ref[0] if count > 1 else 0, out, out_refs, out_sems.at[0])
    grad_low = (grad_gating * gating * (1.0 - gating)).astype(LOW)
    squeeze_low = (low_dot(grad_low, excite[1], ((1,), (1,))) * slope_small).astype(LOW)
    excite_grad[0] = low_dot(squeeze_low, pooled_low, ((0,), (0,)))
    excite_grad[1] = low_dot(act, grad_low, ((0,), (0,)))
    lifts = rows_of(low_dot(squeeze_low, excite[0]) / counts)

    def begin_back(block, carry):

        def wide_strip(index, carry):
            for chunk in range(chunks):
                gain, shift = halves[chunk]
                plain = cross = None
                for part in range(WIDE):
                    place = index * WIDE + part
                    rows = strip_rows(place)
                    code = tiles(codes[middle_rows(place), :])
                    product = tiles(point[rows, col(chunk)])
                    half = product * gain + shift
                    turned = jnp.tanh(half)
                    one = 1.0 + turned
                    slope = 0.5 * (one + half * one * (1.0 - turned))
                    grad = tiles(total[rows, col(chunk)]) * by_segment(code, gates[chunk])
                    lift = jnp.where(code >= 0.0, by_segment(code, lifts[chunk]), 0.0)
                    grad = (grad + lift) * slope
                    residual[rows, col(chunk)] = flat(grad)
                    new = jnp.sum(grad, axis=0)
                    plain = new if plain is None else plain + new
                    new = jnp.sum(grad * product, axis=0)
                    cross = new if cross is None else cross + new
                sums_of[0, :, col(chunk)] += plain
                sums_of[1, :, col(chunk)] += cross
            return carry

        wide_strips_of(block, wide_strip)
        affine_sender.start(block)
        return carry

    sums_of[...] = jnp.zeros(sums_of.shape, F32)
    over_blocks(length, begin_back)
    carries = [[sums_of[i, :, col(chunk)] for i in range(2)] for chunk in range(chunks)]
    gradient_sums(carries, par, copies)
    send_whole(
        [(copies, copies_ref), (excite_grad, excite_grad_ref), (par, par_ref)], last_sems
    )
    for copy in out_copies:
        copy.wait()
    for sender in (res_sender, affine_sender):
        sender.wait_all()


def gradient_sums(carries, par, copies):
    tops, bottoms = [], []
    for chunk, carry in enumerate(carries):
        plain = jnp.sum(carry[0], axis=0, keepdims=True)
        cross = jnp.sum(carry[1], axis=0, keepdims=True)
        mean = par[0:1, col(chunk)]
        tops.append(plain)
        bottoms.append((cross - mean * plain) * par[1:2, col(chunk)])
    write_copies(copies, tops, bottoms)


def back_kernel(halo, layer, share, count, slot, third_slot, me_ref, *rest):
    codes_ref, affine_ref, point_ref, before_ref, matrix_ref = rest[:5]
    rest = rest[5:]
    if layer == 0:
        res_ref, third_ref = rest[:2]
        rest = rest[2:]
    small_refs = rest[:5]
    rest = rest[5:]
    if layer > 0:
        prior_ref = rest[0]
        rest = rest[1:]
    own_ref = rest[0] if halo else None
    rest = rest[1:] if halo else rest
    low_ref, small_ref = rest[:2]
    rest = rest[2:]
    if layer > 0:
        next_ref, copies_ref = rest[:2]
        rest = rest[2:]
    else:
        next_refs, rest = rest[:count], rest[count:]
    codes, affine, point, before, matrix, low, after, buffer, sums, inverse, norm = rest[:11]
    depth, par, small, sums_of, taps = rest[11:16]
    in_sems, out_sems, whole_sems, last_sems = rest[16:20]
    rest = rest[20:]
    own = rest[-1] if halo else None
    length, channels = point_ref.shape
    chunks = channels // LANES
    brought = bring(
        list(small_refs) + [codes_ref], [sums, inverse, norm, depth, par, codes], whole_sems.at[0]
    )
    affine_in = Blocks(affine_ref, affine, in_sems.at[0])
    point_in = Blocks(point_ref, point, in_sems.at[1])
    affine_in.start(0)
    point_in.start(0)
    sources, targets = [of_stack(matrix_ref, slot)], [matrix]
    if layer == 0:
        res, third, lifted = rest[:3]
        sources.append(of_stack(third_ref, third_slot))
        targets.append(third)
    else:
        prior, copies = rest[:2]
        sources.append(prior_ref)
        targets.append(prior)
    if halo:
        sources.append(own_ref)
        targets.append(own)
    later = bring(sources, targets, whole_sems.at[1])
    if layer == 0:
        res_in = Blocks(res_ref, res, in_sems.at[3])
        res_in.start(0)
    for block in range(1, affine_in.count):
        affine_in.start(block)
        point_in.start(block)
        if layer == 0:
            res_in.start(block)
    before_in = Blocks(before_ref, before, in_sems.at[2]).start_all()
    low_sender = Blocks(low, low_ref, out_sems.at[0])
    if layer > 0:
        next_sender = Blocks(after, next_ref, out_sems.at[1])
    for copy in brought[:-1]:
        copy.wait()
    stats = summed(sums)
    inv_total = inverse[0:1, :]
    scale = []
    norm_grads = []
    for chunk in range(chunks):
        plain = stats[chunk : chunk + 1]
        cross = stats[chunks + chunk : chunks + chunk + 1]
        norm_grads.append([cross * share, plain * share])
        mean = par[0:1, col(chunk)]
        inv_std = par[1:2, col(chunk)]
        outer = norm[0, layer : layer + 1, col(chunk)] * inv_std
        slope = outer * inv_std * cross * inv_total
        offset = outer * plain * inv_total - slope * mean
        scale.append((eight(outer), eight(slope), eight(offset)))
    brought[-1].wait()

    def strip(index, carry):
        live = codes[middle_rows(index), :] >= 0.0
        rows = strip_rows(index)
        for chunk in range(chunks):
            outer, slope, offset = scale[chunk]
            value = tiles(affine[rows, col(chunk)]) * outer
            value = value - tiles(point[rows, col(chunk)]) * slope - offset
            low[rows, col(chunk)] = jnp.where(live, flat(value), 0.0).astype(LOW)
        return carry

    def multiply(block):
        rows = block_rows(block)
        grad = rounded(low_dot(low[rows, :], matrix[...], ((1,), (1,))))
        inner = pl.ds(pl.multiple_of(block * BLOCK + EDGE, EDGE), BLOCK)
        for chunk in range(chunks):
            buffer[chunk, inner, :] = grad[:, col(chunk)]
        if layer == 0:
            lift = low_dot(res[rows, :], third[...], ((1,), (1,)))
            for chunk in range(chunks):
                lifted[chunk, rows, :] = lift[:, col(chunk)]

    def block_step(block, carry):
        affine_in.wait(block)
        point_in.wait(block)
        if layer == 0:
            res_in.wait(block - 1)
        multiply(block - 1)
        unrolled_strips_of(block, strip)
        low_sender.start(block)
        return carry

    blocks = length // BLOCK
    affine_in.wait(0)
    point_in.wait(0)
    strips_of(0, strip)
    low_sender.start(0)
    for copy in later:
        copy.wait()
    lax.fori_loop(1, blocks, block_step, 0)
    if layer == 0:
        res_in.wait(blocks - 1)
    multiply(blocks - 1)
    wrap_edges(buffer, chunks, length)
    kinds = 7 if layer > 0 else 5
    sums_of[...] = jnp.zeros(sums_of.shape, F32)
    for k in range(5):
        tap = depth[layer, k : k + 1, :]
        taps[k] = eight(0.5 * tap if layer > 0 else tap)
    if layer > 0:
        taps[5] = eight(prior[2:3, :])
        taps[6] = eight(prior[3:4, :])

    def unmix(block, carry):
        before_in.wait(block)

        def wide_strip(index, carry):
            for chunk in range(chunks):
                kernel = [taps[k, :, col(chunk)] for k in range(5)]
                if layer > 0:
                    gain, shift = taps[5, :, col(chunk)], taps[6, :, col(chunk)]
                found = [None] * kinds
                for part in range(WIDE):
                    place = index * WIDE + part
                    rows = strip_rows(place)
                    value = tiles(buffer[chunk, strip_rows(place, EDGE), :])
                    same = same_utterance(codes, place)
                    terms = [value[k : k + 2] for k in range(5)]
                    for slot, k in enumerate(SIDES):
                        terms[k] = jnp.where(same[slot], terms[k], 0.0)
                    grad = kernel[REACH] * terms[REACH]
                    for k in SIDES:
                        grad = grad + kernel[4 - k] * terms[k]
                    if layer > 0:
                        product = tiles(before[rows, col(chunk)])
                        half = product * gain + shift
                        turned = jnp.tanh(half)
                        one = 1.0 + turned
                        hidden = half * one
                        grad = grad * (one + hidden * (1.0 - turned))
                        hidden = tiles(rounded(flat(hidden)))
                        after[rows, col(chunk)] = flat(grad)
                    else:
                        hidden = tiles(before[rows, col(chunk)].astype(F32))
                        lifted[chunk, rows, :] = flat(grad) + lifted[chunk, rows, :]
                    if own is not None:
                        inside = tiles(own[rows, :])
                        hidden = hidden * inside
                        grad = grad * inside
                    new = [jnp.sum(hidden * terms[4 - k], axis=0) for k in range(5)]
                    if layer > 0:
                        new += [jnp.sum(grad, axis=0), jnp.sum(grad * product, axis=0)]
                    found = [b if a is None else a + b for a, b in zip(found, new, strict=True)]
                for k in range(kinds):
                    sums_of[k, :, col(chunk)] += found[k]
            return carry

        wide_strips_of(block, wide_strip)
        if layer > 0:
            next_sender.start(block)
        return carry

    over_blocks(length, unmix)
    if layer == 0:
        out_of_order(lifted, after, chunks, length, 0)
        me = me_ref[0] if count > 1 else 0
        piece_copies = send_pieces(me, after, next_refs, out_sems.at[1])
    for chunk in range(chunks):
        tile = [jnp.sum(sums_of[k, :, col(chunk)], axis=0, keepdims=True) for k in range(5)]
        tile += norm_grads[chunk] + [jnp.zeros((SEGROWS - 7, LANES), F32)]
        small[:, col(chunk)] = jnp.concatenate(tile, axis=0).astype(LOW)
    pairs = [(small, small_ref)]
    if layer > 0:
        carries = [[sums_of[5 + i, :, col(chunk)] for i in range(2)] for chunk in range(chunks)]
        gradient_sums(carries, prior, copies)
        pairs.append((copies, copies_ref))
    send_whole(pairs, last_sems)
    low_sender.wait_all()
    if layer > 0:
        next_sender.wait_all()
    else:
        for copy in piece_copies:
            copy.wait()


def run(body, me, args, outs, scratch, flops=0):
    there = pl.BlockSpec(memory_space=pl.ANY)
    first = [pl.BlockSpec(memory_space=pltpu.SMEM)] * len(me)
    moved = sum(a.size * a.dtype.itemsize for a in args)
    return pl.pallas_call(
        body,
        out_shape=[jax.ShapeDtypeStruct(shape, dtype) for shape, dtype in outs],
        in_specs=first + [there] * len(args),
        out_specs=[there] * len(outs),
        scratch_shapes=[
            piece if not isinstance(piece, tuple) else pltpu.VMEM(*piece) for piece in scratch
        ],
        compiler_params=pltpu.CompilerParams(vmem_limit_bytes=SCOPED),
        cost_estimate=pl.CostEstimate(flops=flops, bytes_accessed=moved, transcendentals=0),
    )(*me, *args)


def close(value):
    return pltpu.with_memory_space_constraint(value, pltpu.VMEM)


def exchange(blocks, axis):
    return lax.all_to_all(blocks, axis, 0, 0)


def copies_of(block, count):
    return jnp.broadcast_to(block[None], (count,) + block.shape)


def swish_slope(value):
    sigma = jax.nn.sigmoid(value)
    return sigma * (1.0 + value * (1.0 - sigma))


def lamb_terms(weights, first, second, grads):
    first_new = BETA_ONE * first + (1.0 - BETA_ONE) * grads
    second_new = BETA_TWO * second + (1.0 - BETA_TWO) * grads * grads
    first_hat = first_new / (1.0 - BETA_ONE**STEP)
    second_hat = second_new / (1.0 - BETA_TWO**STEP)
    update = first_hat / (jnp.sqrt(second_hat) + LAMB_EPS) + DECAY * weights
    return (first_new, second_new, update)


def finish_kernel(small_rows, *refs):
    gathered, weights, updates = refs[:3]
    depth, norm, excite = refs[3:6], refs[6:9], refs[9:12]
    new_ref, half_ref = refs[12:14]
    depth_out, norm_out, excite_out = refs[14:17], refs[17:20], refs[20:23]
    trust_ref, rows, spread = refs[23:]
    each = small_rows + 1
    matrices = weights.shape[0]
    convs, taps = depth[0].shape[:2]
    rows[...] = gathered[...].astype(F32)

    def row(index):
        place = index // small_rows * each + index % small_rows
        return rows[place : place + 1, :]

    squares = rows[small_rows : small_rows + 1, :]
    for device in range(1, gathered.shape[0] // each):
        place = device * each + small_rows
        squares = squares + rows[place : place + 1, :]
    squares = squares[:, col(0)] + squares[:, col(1)] + squares[:, col(2)]
    norms = [
        (jnp.sqrt(squares[:, m : m + 1]), jnp.sqrt(squares[:, matrices + m : matrices + m + 1]))
        for m in range(matrices)
    ]
    for m, (weight_norm, update_norm) in enumerate(norms):
        new = weights[m] - RATE * (weight_norm / update_norm) * updates[m]
        new_ref[m] = new
        half_ref[m] = new.astype(LOW)

    def total(value):
        return jnp.sum(jnp.sum(value, axis=1, keepdims=True), axis=0, keepdims=True)

    def step(old, grad):
        first, second, update = lamb_terms(*old, grad)
        weight_norm = jnp.sqrt(total(old[0] * old[0]))
        update_norm = jnp.sqrt(total(update * update))
        new = old[0] - RATE * (weight_norm / update_norm) * update
        return (first, second, new), (weight_norm, update_norm)

    sides = [[], []]
    for layer in range(convs):
        base = layer * SEGROWS
        grad = jnp.concatenate([row(base + k) for k in range(taps)], axis=0)
        results, pair = step([ref[layer] for ref in depth], grad)
        for ref, result in zip(depth_out, results, strict=True):
            ref[layer] = result
        norms.append(pair)
        for side in range(2):
            old = [ref[layer, side : side + 1, :] for ref in norm]
            results, pair = step(old, row(base + taps + side))
            for ref, result in zip(norm_out, results, strict=True):
                ref[layer, side : side + 1, :] = result
            sides[side].append(pair)
    norms += sides[0] + sides[1]
    base = convs * SEGROWS
    for index in range(spread.shape[0]):
        spread[index : index + 1, :] = row(base + index)
    size = excite[0].shape[1]
    for side in range(2):
        grad = spread[side * size : (side + 1) * size, :]
        results, pair = step([ref[side] for ref in excite], grad)
        for ref, result in zip(excite_out, results, strict=True):
            ref[side] = result
        norms.append(pair)
    lane = lax.broadcasted_iota(jnp.int32, (1, LANES), 1)
    for side in range(2):
        line = jnp.zeros((1, LANES), F32)
        for index, pair in enumerate(norms):
            line = jnp.where(lane == index, pair[side], line)
        trust_ref[side : side + 1, :] = line[:, : len(norms)]


def local_lamb(weights, first, second, grads, axes):
    first_new, second_new, update = lamb_terms(weights, first, second, grads)
    weight_norm = jnp.sqrt(jnp.sum(weights * weights, axis=axes, keepdims=True))
    update_norm = jnp.sqrt(jnp.sum(update * update, axis=axes, keepdims=True))
    weights_new = weights - RATE * (weight_norm / update_norm) * update
    return (first_new, second_new, weights_new, weight_norm.reshape(-1), update_norm.reshape(-1))


def local(
    inputs,
    utterance_ids,
    cotangent,
    pointwise,
    pointwise_first,
    pointwise_second,
    depthwise,
    depthwise_first,
    depthwise_second,
    norm_affine,
    norm_first,
    norm_second,
    excite_mats,
    excite_first,
    excite_second,
):
    batches, _, frames, channels = inputs.shape
    convs, taps = depthwise.shape[:2]
    matrices, shard_rows = pointwise.shape[:2]
    chunks = channels // LANES
    across_dp = lax.axis_size("dp")
    across_tm = lax.axis_size("tm")
    parts = across_tm // batches
    own = frames * batches
    width = BLOCK // 2 if parts > 1 else 0
    length = own + 2 * width
    groups = None
    partners = None
    if parts > 1:
        groups = [[part * batches + b for b in range(batches)] for part in range(parts)]
        partners = [[part * batches + b for part in range(parts)] for b in range(batches)]

    def over_rows(block):
        return lax.all_to_all(block, "tm", 0, 0, axis_index_groups=groups)

    def to_next(piece, step):
        return lax.ppermute(piece, "tm", [(i, (i + step) % batches) for i in range(batches)])

    def with_permutes(pieces):
        return pieces[:1] + [to_next(pieces[k], k) for k in range(1, batches)]

    def step_pieces(block):
        if parts > 1:
            return [over_rows(block)]
        return with_permutes(
            [
                lax.dynamic_index_in_dim(block, lax.rem(me + step, batches), 0, keepdims=False)
                for step in range(batches)
            ]
        )

    def settle(pieces):
        if parts > 1:
            return pieces[0]
        placed = []
        for source in range(batches):
            distance = lax.rem(me - source + batches, batches)
            piece = pieces[0]
            for step in range(1, batches):
                piece = jnp.where(distance == step, pieces[step], piece)
            placed.append(piece)
        return jnp.stack(placed)

    def over_parts(value):
        if parts == 1:
            return value
        return lax.psum(value, "tm", axis_index_groups=partners)

    def with_neighbours(block):
        if parts == 1:
            return block
        forward = [(i, i + batches) for i in range(across_tm - batches)]
        backward = [(target, source) for source, target in forward]
        before = lax.ppermute(block[-width:], "tm", forward)
        after = lax.ppermute(block[:width], "tm", backward)
        return jnp.concatenate([block, after, before], axis=0)

    def own_sums(copies):
        if parts > 1:
            copies = copies_of(over_parts(copies[0]), across_dp)
        sums = exchange(copies, "dp")
        return close(sums) if parts == 1 else sums

    me = lax.axis_index("tm")
    id_rows = -(-frames // channels)
    ids_low = jnp.pad(utterance_ids[:, 0], ((0, 0), (0, id_rows * channels - frames)))
    ids_low = ids_low.astype(LOW).reshape(batches, id_rows, channels)
    both = copies_of(pointwise[:2].astype(LOW).reshape(2 * shard_rows, channels), across_tm)
    early = exchange(jnp.concatenate([both, jnp.concatenate([ids_low] * parts, axis=0)], axis=1), "tm")
    early, x_held = lax.optimization_barrier((early, inputs))
    if parts == 1:
        first = lax.dynamic_index_in_dim(inputs[:, 0], lax.rem(me + 1, batches), 0, keepdims=False)
        x_pieces = step_pieces(x_held[:, 0])
        x_pieces[1] = to_next(first, 1)
    else:
        x_pieces = [with_neighbours(over_rows(x_held[:, 0]).reshape(own, channels))]
    ids_own = early[:, 2 * shard_rows : 2 * shard_rows + id_rows].reshape(across_tm, -1)[:, :frames]
    if parts > 1:
        ids_own = lax.dynamic_slice_in_dim(ids_own, me // batches * batches, batches, 0)
    ids_own = ids_own.astype(jnp.int32).reshape(own)
    late = lax.all_gather(pointwise[2:].astype(LOW), ("dp", "tm"), axis=1, tiled=True)
    excite_low = excite_mats.astype(LOW)
    ids = with_neighbours(ids_own[:, None] + 1)[:, 0] - 1
    run_length = length // ROWS8
    place = jnp.arange(length, dtype=jnp.int32)
    code = jnp.where(ids >= 0, ids, -2 - place).astype(F32)
    if parts == 1:
        head = (-2 - length - jnp.arange(REACH, dtype=jnp.int32)).astype(F32)
        tail = head - REACH
    else:
        head, tail = code[-REACH:], code[:REACH]
    code = jnp.concatenate([head, code, tail])
    code = jnp.stack(
        [code[s * run_length : (s + 1) * run_length + 2 * REACH] for s in range(ROWS8)], axis=1
    )
    codes = jnp.broadcast_to(code.reshape(-1)[:, None], (length + 2 * EDGE, LANES))

    early = [
        early[:, i * shard_rows : (i + 1) * shard_rows].reshape(-1, channels) for i in range(2)
    ]
    early[0] = lax.all_gather(early[0], "dp", tiled=True)
    early[0], early[1], codes = lax.optimization_barrier((early[0], early[1], codes))
    early[1] = lax.all_gather(early[1], "dp", tiled=True)
    x_pieces[0], early = lax.optimization_barrier((x_pieces[0], early))

    def in_order(values):
        return jnp.swapaxes(values.reshape((ROWS8, run_length) + values.shape[1:]), 0, 1).reshape(
            values.shape
        )

    def in_time(values):
        return jnp.swapaxes(values.reshape((run_length, ROWS8) + values.shape[1:]), 0, 1).reshape(
            values.shape
        )

    ids_order = in_order(ids)
    own_order = in_order(place) < own
    halo = [jnp.broadcast_to(own_order.astype(F32)[:, None], (length, LANES))] if parts > 1 else []
    wide = (length, channels)
    blocks = length // BLOCK
    code_shape = (codes.shape, F32)
    buffer = ((chunks, length + 2 * EDGE, LANES), F32)
    split = ((chunks, length, LANES), F32)
    square = ((channels, channels), LOW)
    copies = ((across_dp, 2 * chunks, LANES), F32)
    par = ((ROWS8, channels), F32)
    product = 2 * length * channels * channels

    def sems(*shape):
        return pltpu.SemaphoreType.DMA(shape)

    here = [me.astype(jnp.int32).reshape(1)]
    norm_shape, depth_shape = (norm_affine.shape, F32), (depthwise.shape, F32)
    tile_shape = ((ROWS8, LANES), F32)
    own_shape = [((length, LANES), F32)] * len(halo)
    mixed, points, pars = [None] * convs, [None] * convs, [None] * convs
    forward_scratch = [((taps, ROWS8, channels), F32), square, (wide, LOW), (wide, F32), buffer]
    first_copies = ((across_dp, 2 * ROWS8, LANES), F32)
    weights = early + [None] * (matrices - 2)
    slots = [None, None] + list(range(matrices - 2))
    mixed[0], points[0], x_order, sums = run(
        functools.partial(first_kernel, bool(halo), len(x_pieces)),
        here,
        [close(piece) if parts == 1 else piece for piece in x_pieces]
        + [codes, weights[0], depthwise]
        + halo,
        [(wide, LOW), (wide, F32), (wide, LOW), first_copies],
        [(wide, LOW), code_shape, (wide, LOW), depth_shape, first_copies]
        + forward_scratch
        + [sems(blocks), sems(3, blocks), sems(4), sems(1)]
        + own_shape,
        product,
    )
    weights[2:] = [late] * (matrices - 2)
    sums = own_sums(sums)
    inverse = []
    for layer in range(convs - 1):
        extra = [tile_shape] if layer == 0 else []
        result = run(
            functools.partial(next_kernel, bool(halo), layer, slots[layer + 1]),
            [],
            [codes, points[layer], weights[layer + 1], sums, norm_affine, depthwise]
            + inverse
            + halo,
            [(wide, LOW), (wide, F32), copies, par] + extra,
            [code_shape, (wide, F32), (sums.shape, F32), tile_shape, norm_shape, par]
            + [depth_shape, copies]
            + forward_scratch
            + [sems(blocks), sems(2, blocks), sems(2, 4), sems(3)]
            + own_shape,
            product,
        )
        mixed[layer + 1], points[layer + 1], sums, pars[layer] = result[:4]
        if layer == 0:
            inverse = [result[4]]
            cot_held, sums = lax.optimization_barrier((cotangent, sums))
            cot_pieces = step_pieces(cot_held[:, 0])
        sums = own_sums(sums)
    last = convs - 1
    if parts == 1:
        excite_shape = (excite_mats.shape, F32)
        piece = ((frames, channels), LOW)
        result = run(
            functools.partial(excite_kernel, last, len(cot_pieces), slots[convs]),
            here,
            [close(piece) for piece in cot_pieces]
            + [codes, points[last], x_order, weights[convs], sums, inverse[0], norm_affine]
            + [excite_low],
            [piece] * batches + [(wide, LOW), (wide, F32), copies, excite_shape, par],
            [code_shape, (wide, F32), (wide, LOW), (wide, LOW), square, copies, tile_shape]
            + [norm_shape, (excite_low.shape, LOW)]
            + [(wide, F32)] * 3
            + [split]
            + [(wide, LOW)] * 2
            + [copies, excite_shape, par, ((SEGROWS, channels), F32)]
            + [((ROWS8, ROWS8, channels), F32)]
            + [sems(3, blocks), sems(3, blocks), sems(2, 4), sems(3)],
            product,
        )
        out_pieces = with_permutes(list(result[:batches]))
        grad_res, affine, sums, excite_grad, pars[last] = result[batches:]
    else:
        stats = jnp.sum(sums, axis=0).reshape(2, channels)
        mean = stats[0] * inverse[0][0, 0]
        inv_std = lax.rsqrt(stats[1] * inverse[0][0, 0] - mean * mean + BN_EPS)
        gain = norm_affine[0, last] * inv_std
        shift = norm_affine[1, last] - mean * gain
        pars[last] = jnp.pad(jnp.stack([mean, inv_std, 0.5 * gain, 0.5 * shift]), ((0, 4), (0, 0)))
        mask = (ids_order >= 0).astype(F32)[:, None]
        own_mask = own_order.astype(F32)[:, None]
        value = points[last] * gain + shift
        hidden = value * jax.nn.sigmoid(value) * mask
        segment_index = jnp.arange(SEGROWS, dtype=jnp.int32)
        onehot = ids_order[None, :] == jnp.where(segment_index < NSEG, segment_index, -9)[:, None]
        onehot = onehot.astype(F32)

        def gather(values):
            values = jnp.dot(onehot, values * own_mask, precision=lax.Precision.HIGHEST)
            return over_parts(values)

        def pick(values):
            return jnp.dot(onehot.T, values, precision=lax.Precision.HIGHEST)

        count = over_parts(jnp.dot(onehot, own_mask, precision=lax.Precision.HIGHEST))
        count = jnp.where(segment_index < NSEG, count[:, 0], 1.0)[:, None]
        pooled_low, slope_small, act, gating = squeeze_forward(gather(hidden), count, excite_low)
        spread = pick(gating)
        total = hidden * spread + low_dot(x_order, weights[convs][slots[convs]])
        block_out = in_time((total * jax.nn.sigmoid(total) * mask).astype(LOW))
        out_pieces = [over_rows(block_out[:own].reshape(batches, frames, channels))]
        cot_low = with_neighbours(cot_pieces[0].reshape(own, channels))
        grad_total = in_order(cot_low).astype(F32) * mask * swish_slope(total)
        grad_res = grad_total.astype(LOW)
        grad_low = (gather(grad_total * hidden) * gating * (1.0 - gating)).astype(LOW)
        squeeze_low = (low_dot(grad_low, excite_low[1], ((1,), (1,))) * slope_small).astype(LOW)
        excite_grad = jnp.stack(
            [
                low_dot(squeeze_low, pooled_low, ((0,), (0,))),
                low_dot(act, grad_low, ((0,), (0,))),
            ]
        )
        affine = grad_total * spread + pick(low_dot(squeeze_low, excite_low[0]) / count)
        affine = affine * swish_slope(value)
        plain = jnp.sum(affine * own_mask, axis=0)
        cross = jnp.sum(affine * own_mask * (points[last] - mean) * inv_std, axis=0)
        sums = copies_of(jnp.stack([plain, cross]).reshape(2 * chunks, LANES), across_dp)

    def weight_grad(left, right):
        if parts > 1:
            left = left * own_order.astype(LOW)[:, None]
        return low_dot(left, right, ((0,), (0,)))

    def to_row(grads):
        grads = grads.astype(LOW)
        return lax.psum_scatter(grads, "dp", scatter_dimension=1, tiled=True)

    share = 1.0 / (across_dp * parts)
    point_grads = [None] * matrices
    point_grads[convs] = weight_grad(x_order, grad_res)
    small_grads = [None] * convs
    small_tile = ((SEGROWS, channels), LOW)
    for layer in reversed(range(convs)):
        sums = own_sums(sums)
        arrived = convs - 2 - layer
        if 0 < arrived < len(out_pieces):
            sums, out_pieces[arrived] = lax.optimization_barrier((sums, out_pieces[arrived]))
        near_args = [sums, inverse[0], norm_affine, depthwise, pars[layer]]
        scratch = [code_shape, (wide, F32), (wide, F32), None, square, (wide, LOW), None, buffer]
        scratch += [copies, tile_shape, norm_shape, depth_shape, par, small_tile]
        scratch += [((ROWS8, ROWS8, channels), F32)] * 2
        args = [codes, affine, points[layer]]
        if layer > 0:
            args += [points[layer - 1], weights[layer]] + near_args + [pars[layer - 1]]
            scratch[3], scratch[6] = (wide, F32), (wide, F32)
            scratch += [sems(3, blocks), sems(2, blocks), sems(2, 6), sems(2), par, copies]
            outs = [(wide, LOW), small_tile, (wide, F32), copies]
        else:
            args += [x_order, weights[layer], grad_res, weights[convs]] + near_args
            scratch[3], scratch[6] = (wide, LOW), (wide, LOW)
            scratch += [sems(4, blocks), sems(3, blocks), sems(2, 6), sems(2)]
            scratch += [(wide, LOW), square, split]
            outs = [(wide, LOW), small_tile]
            whole = ((frames, channels), LOW)
            outs += [(wide, LOW)] if parts > 1 else [whole] * batches
        result = run(
            functools.partial(
                back_kernel,
                bool(halo),
                layer,
                share,
                batches if parts == 1 else 1,
                slots[layer],
                slots[convs],
            ),
            here,
            args + halo,
            outs,
            scratch + own_shape,
            2 * product,
        )
        grad_low, small_grads[layer] = result[:2]
        if layer > 0:
            affine, sums = result[2:]
        point_grads[layer] = weight_grad(mixed[layer], grad_low)
        if layer == convs - 1:
            sent = [to_row(jnp.stack([point_grads[layer], point_grads[convs]]))]
        elif layer == 2:
            sent.append(to_row(jnp.stack([point_grads[2], point_grads[3]])))
    if parts == 1:
        in_pieces = with_permutes(list(result[2:]))
    else:
        in_pieces = [over_rows(result[2][:own].reshape(batches, frames, channels))]

    devices = across_dp * across_tm
    excite_low = (excite_grad.reshape(-1, channels) * (1.0 / parts)).astype(LOW)
    small = jnp.concatenate(small_grads + [excite_low], axis=0)
    small_rows = -(-small.shape[0] // devices)
    small = jnp.pad(small, ((0, small_rows * devices - small.shape[0]), (0, 0)))
    send = jnp.concatenate(
        [g.reshape(across_dp, -1, channels).astype(LOW) for g in point_grads[:2]]
        + [small.reshape(across_dp, -1, channels)],
        axis=1,
    )
    held = jnp.sum(exchange(send, "dp").astype(F32), axis=0)
    big = 2 * across_tm * shard_rows
    point_all = jnp.concatenate(
        [held[:big].reshape(2, across_tm, shard_rows, channels)]
        + [part.reshape(-1, across_tm, shard_rows, channels) for part in sent[::-1]],
        axis=0,
    ).astype(LOW)
    send = jnp.concatenate(
        [
            jnp.transpose(point_all, (1, 0, 2, 3)).reshape(across_tm, -1, channels),
            held[big:].reshape(across_tm, -1, channels).astype(LOW),
        ],
        axis=1,
    )
    send, in_pieces[1::2] = lax.optimization_barrier((send, in_pieces[1::2]))
    held = jnp.sum(exchange(send, "tm").astype(F32), axis=0)
    input_grad = settle(in_pieces).astype(F32)
    block_out = settle(out_pieces)
    point_shard = held[: matrices * shard_rows].reshape(pointwise.shape)
    small_shard = held[matrices * shard_rows :]

    pw_moment, pw_square, pw_update = lamb_terms(
        pointwise, pointwise_first, pointwise_second, point_shard
    )
    squares = jnp.concatenate(
        [
            jnp.sum(pointwise * pointwise, axis=(1, 2)),
            jnp.sum(pw_update * pw_update, axis=(1, 2)),
        ]
    )
    squares = three_parts(squares[None])
    squares = jnp.pad(squares, ((0, 0), (0, LANES - squares.shape[1]))).reshape(1, -1)
    squares = jnp.pad(squares, ((0, 0), (0, channels - squares.shape[1])))
    everything = exchange(
        copies_of(jnp.concatenate([small_shard.astype(LOW), squares], axis=0), devices),
        ("dp", "tm"),
    )
    if parts == 1:

        def turned(value):
            return jnp.transpose(value, (1, 0, 2))

        depth = [depthwise, depthwise_first, depthwise_second]
        norm = [turned(value) for value in (norm_affine, norm_first, norm_second)]
        excite = [excite_mats, excite_first, excite_second]
        tensors = depth + norm + excite
        everything = everything.reshape(-1, channels)
        shapes = [(pointwise.shape, F32), (pointwise.shape, LOW)]
        shapes += [(value.shape, F32) for value in tensors]
        count = matrices + 3 * convs + excite_mats.shape[0]
        result = pl.pallas_call(
            functools.partial(finish_kernel, small_rows),
            out_shape=[
                jax.ShapeDtypeStruct(shape, dtype) for shape, dtype in shapes + [((2, count), F32)]
            ],
            scratch_shapes=[
                pltpu.VMEM(everything.shape, F32),
                pltpu.VMEM((2 * excite_mats.shape[1], channels), F32),
            ],
            compiler_params=pltpu.CompilerParams(vmem_limit_bytes=SCOPED),
        )(close(everything), pointwise, pw_update, *tensors)
        pw_new, pw_half = result[:2]
        return (
            block_out[:, None],
            input_grad[:, None],
            pw_moment,
            pw_square,
            pw_new,
            pw_half,
            *result[2:5],
            *[turned(value) for value in result[5:8]],
            *result[8:11],
            result[11],
        )
    everything = everything.astype(F32)
    squares = jnp.sum(everything[:, small_rows].reshape(devices, -1, LANES), axis=(0, 1))
    small = everything[:, :small_rows].reshape(-1, channels)
    cut = convs * SEGROWS
    by_layer = small[:cut].reshape(convs, SEGROWS, channels)
    grad_depth = by_layer[:, :taps]
    grad_norm = jnp.transpose(by_layer[:, taps : taps + 2], (1, 0, 2))
    grad_excite = small[cut : cut + 2 * excite_mats.shape[1]].reshape(excite_mats.shape)
    pw_wn = jnp.sqrt(squares[:matrices])
    pw_un = jnp.sqrt(squares[matrices : 2 * matrices])
    pw_new = pointwise - RATE * (pw_wn / pw_un)[:, None, None] * pw_update
    dw_moment, dw_square, dw_new, dw_wn, dw_un = local_lamb(
        depthwise, depthwise_first, depthwise_second, grad_depth, (1, 2)
    )
    nm_moment, nm_square, nm_new, nm_wn, nm_un = local_lamb(
        norm_affine, norm_first, norm_second, grad_norm, (2,)
    )
    se_moment, se_square, se_new, se_wn, se_un = local_lamb(
        excite_mats, excite_first, excite_second, grad_excite, (1, 2)
    )
    trust_norms = jnp.stack(
        [
            jnp.concatenate([pw_wn, dw_wn, nm_wn, se_wn]),
            jnp.concatenate([pw_un, dw_un, nm_un, se_un]),
        ]
    )
    return (
        block_out[:, None],
        input_grad[:, None],
        pw_moment,
        pw_square,
        pw_new,
        pw_new.astype(LOW),
        dw_moment,
        dw_square,
        dw_new,
        nm_moment,
        nm_square,
        nm_new,
        se_moment,
        se_square,
        se_new,
        trust_norms,
    )


def solution(mesh):
    rows = P(None, "dp", "tm", None)
    shards = P(None, ("dp", "tm"), None)
    return jax.shard_map(
        local,
        mesh=mesh,
        in_specs=(rows, P(None, "dp", "tm"), rows, shards, shards, shards) + (P(),) * 9,
        out_specs=(rows, rows, shards, shards, shards, shards) + (P(),) * 10,
        check_vma=False,
    )
```
